32 devices in a mesh: ladder: 8 (over z, y), gx: 4 (over x, core).
Axes of the slice: x: 2, y: 2, z: 4, core: 2. Of those that a mesh axis runs over, the one named last changes fastest.
Arguments:
- field: float32 [8, 24, 96, 768], P('ladder', 'gx'), may hold values from -1.1 to 2.7
- momenta: float32 [8, 24, 96, 768], P('ladder', 'gx'), may hold values from -4 to 4
- kappas: float32 [8], replicated, may hold values from 0.1 to 0.112, as said below
- partner: int32 [8], replicated, may hold values from 0 to 7, as said below
Outputs:
- field_out: float32 [8, 24, 96, 768], P('ladder', 'gx')
- momenta_out: float32 [8, 24, 96, 768], P('ladder', 'gx')
- stats: float32 [8, 5], P('ladder')
The draws below stay inside these ranges and needn't reach their ends.
Inputs may be any that keep to these rules, and one draw needn't show every extreme that they name: partner[partner[r]] = r; each entry is r - 1, r or r + 1; the swapping pairs all begin at indices of one parity; at least one pair swaps. kappas rise strictly along the ladder.
All inputs are finite; a program needn't handle non-finite values.
Results may differ from the reference program's by a relative error of at most 0.00002.
Values sent between devices are 32-bit elements; how exact they have to be, the bound alone decides.
A program may use at most 128 MiB of HBM per device.

```python
import jax
import jax.numpy as jnp
from jax import lax

NY = 96
NZ = 96
NT = 8
LEAPS = 4
NX = 24
NL = 8


def draw_field(key, part):
    first = jax.random.fold_in(key, 0)
    shape = (NL, NX, NY, NZ * NT)
    slope = 0.4 + 0.8 * jnp.arange(NX, dtype=jnp.float32) / (NX - 1)
    rough = 0.5 * jax.random.truncated_normal(first, -3.0, 3.0, shape, jnp.float32)
    return slope[None, :, None, None] + rough


def draw_kappas(key, part):
    jitter = jax.random.uniform(key, (NL,), jnp.float32)
    return 0.1 + 0.0015 * (jnp.arange(NL, dtype=jnp.float32) + 0.45 * jitter)


def draw_partner(key, part):
    first, second = jax.random.split(jax.random.fold_in(key, 7))
    parity = jax.random.randint(first, (), 0, 2)
    accept = jax.random.randint(second, (NL,), 0, 4) > 0
    index = jnp.arange(NL, dtype=jnp.int32)
    accept = jnp.where(index == parity, True, accept)
    lower = (index % 2 == parity) & (index + 1 < NL) & accept
    upper = jnp.roll(lower, 1) & (index > 0)
    return (index + lower.astype(jnp.int32) - upper.astype(jnp.int32)).astype(jnp.int32)


def levels(key, shape, cuts, least, largest):
    def one(axis_at, parts):
        heights = jax.random.uniform(jax.random.fold_in(jax.random.fold_in(key, 6), axis_at), (parts,), jnp.float32, least / len(cuts), largest / len(cuts))
        return jnp.repeat(jnp.exp(heights), shape[axis_at] // parts).reshape((-1,) + (1,) * (len(shape) - axis_at - 1))

    level = one(*cuts[0])
    for cut in cuts[1:]:
        level = level * one(*cut)
    return level


def scatter_about(rng, shape, spread, limit, shards=(), held_as=jnp.bfloat16):
    result = spread * jax.random.normal(rng, shape, jnp.float32)
    if shards:
        result = result * levels(rng, shape, shards, -0.22, 0.18)
    return jnp.clip(result, -limit, limit).astype(held_as)


def setup_inputs(seed: int = 0) -> dict:
    keys = jax.random.split(jax.random.key(seed), 5)
    return {
        "field": draw_field(jax.random.fold_in(keys[4], 71), 0),
        "momenta": scatter_about(keys[1], (NL, NX, NY, NZ * NT), 1.0, 4.0, ((0, 8), (1, 4)), jnp.float32),
        "kappas": draw_kappas(jax.random.fold_in(keys[4], 71), 0),
        "partner": draw_partner(jax.random.fold_in(keys[4], 71), 0),
    }


LAMBDA = 0.5
STEP = 0.1


def time_roll(arr, by):
    slot = jnp.arange(arr.shape[-1], dtype=jnp.int32) % NT
    main = jnp.roll(arr, by, -1)
    if by > 0:
        other = jnp.roll(arr, by - NT, -1)
        return jnp.where(slot == 0, other, main)
    other = jnp.roll(arr, by + NT, -1)
    return jnp.where(slot == NT - 1, other, main)


def neighbours(field):
    total = jnp.roll(field, 1, 0) + jnp.roll(field, -1, 0)
    total = total + jnp.roll(field, 1, 1) + jnp.roll(field, -1, 1)
    total = total + jnp.roll(field, NT, 2) + jnp.roll(field, -NT, 2)
    return total + time_roll(field, 1) + time_roll(field, -1)


def force(field, kappa):
    square = field * field
    return 2.0 * kappa * neighbours(field) - 2.0 * field - 4.0 * LAMBDA * (square - 1.0) * field


def site_sums(field, moment):
    ahead = jnp.roll(field, -1, 0) + jnp.roll(field, -1, 1) + jnp.roll(field, -NT, 2) + time_roll(field, -1)
    square = field * field
    hop = jnp.sum(field * ahead)
    pot = jnp.sum(square + LAMBDA * (square - 1.0) ** 2)
    kin = 0.5 * jnp.sum(moment * moment)
    return hop, pot, kin


def evolve(items):
    field, moment, kappa = items
    volume = field.size
    hop0, pot0, kin0 = site_sums(field, moment)
    energy = kin0 / volume + pot0 / volume - 2.0 * kappa * (hop0 / volume)
    moment = moment + 0.5 * STEP * force(field, kappa)
    for leap in range(LEAPS):
        field = field + STEP * moment
        scale = STEP if leap < LEAPS - 1 else 0.5 * STEP
        moment = moment + scale * force(field, kappa)
    hop1, pot1, kin1 = site_sums(field, moment)
    values = jnp.stack([hop1 / volume, pot1 / volume, kin1 / volume, energy])
    return field, moment, values


def reference(field, momenta, kappas, partner):
    fields, moments, values = lax.map(evolve, (field, momenta, kappas))
    field_out = jnp.take(fields, partner, axis=0)
    momenta_out = jnp.take(moments, partner, axis=0)
    gaps = jnp.concatenate([kappas[1:] - kappas[:-1], jnp.zeros((1,), jnp.float32)])
    span = kappas[-1] - kappas[0]
    terms = 2.0 * values[:, 0] * gaps / span
    cumulative = jnp.cumsum(terms)
    stats = jnp.concatenate([values, cumulative[:, None]], axis=1)
    return field_out, momenta_out, stats
```

```python
import functools

import jax
import jax.numpy as jnp
from jax import lax
from jax.experimental import pallas as pl
from jax.experimental.pallas import tpu as pltpu
from jax.sharding import PartitionSpec as P

NT = 8
LEAPS = 4
LAMBDA = 0.5
STEP = 0.1

ROWS = 16
LAG = 2
STAGES = LEAPS + 1
LANES = 128
MESH = pl.DeviceIdType.MESH


def shifted_t(tile, slot):
    ahead = jnp.where(slot == NT - 1, pltpu.roll(tile, NT - 1, 1), pltpu.roll(tile, LANES - 1, 1))
    behind = jnp.where(slot == 0, pltpu.roll(tile, LANES - NT + 1, 1), pltpu.roll(tile, 1, 1))
    return ahead + behind


def zt_sum(cur, lane, slot):
    count = cur.shape[1] // LANES
    tiles = [cur[:, k * LANES : (k + 1) * LANES] for k in range(count)]
    up = [pltpu.roll(t, NT, 1) for t in tiles]
    down = [pltpu.roll(t, LANES - NT, 1) for t in tiles]
    sums = []
    for k in range(count):
        below = jnp.where(lane < NT, up[k - 1], up[k])
        above = jnp.where(lane >= LANES - NT, down[(k + 1) % count], down[k])
        sums.append(below + above + shifted_t(tiles[k], slot))
    return jnp.concatenate(sums, axis=1)


def fold(block):
    total = block[:, :LANES]
    for k in range(1, block.shape[1] // LANES):
        total = total + block[:, k * LANES : (k + 1) * LANES]
    return total


def body(
    odd, ring, rungs, kappas, partner, field, momenta,
    field_out, momenta_out, stats,
    fb, pb, halo, got_f, got_p, acc, own, gx_buf, rung_buf,
    load_sem, halo_send, halo_recv, swap_send, swap_recv, out_sem,
    gx_send, gx_recv, rung_send, rung_recv,
):
    planes, height, width = pb.shape
    chunks = height // ROWS
    rung = lax.axis_index("ladder")
    me = lax.axis_index("gx")
    right = lax.rem(me + 1, ring)
    left = lax.rem(me + ring - 1, ring)
    even_place = lax.rem(rung, 2) == 0
    if odd:
        paired = (rung > 0) & (rung < rungs - 1)
        mate = jnp.where(even_place, rung - 1, rung + 1)
        mate = jnp.where(paired, mate, rung)
    else:
        paired = None
        mate = jnp.where(even_place, rung + 1, rung - 1)

    def when_paired(todo):
        if odd:
            pl.when(paired)(todo)
        else:
            todo()

    loads = [
        pltpu.make_async_copy(field.at[0], fb.at[0], load_sem.at[0]),
        pltpu.make_async_copy(momenta.at[0], pb, load_sem.at[1]),
    ]
    for load in loads:
        load.start()

    barrier = pltpu.get_barrier_semaphore()
    for off in range(1, ring):
        pl.semaphore_signal(barrier, inc=1, device_id=(rung, lax.rem(me + off, ring)), device_id_type=MESH)
    for off in range(1, rungs):
        pl.semaphore_signal(barrier, inc=1, device_id=(lax.rem(rung + off, rungs), me), device_id_type=MESH)
    pl.semaphore_wait(barrier, ring - 1 + rungs - 1)

    def span(c):
        return pl.ds(pl.multiple_of(c * ROWS, ROWS), ROWS)

    def halo_copies(stage, c):
        rows = span(c)
        if stage == 0:
            low, high = field.at[0, 0, rows], field.at[0, planes - 1, rows]
        else:
            low, high = fb.at[stage, 0, rows], fb.at[stage, planes - 1, rows]
        down = pltpu.make_async_remote_copy(
            src_ref=low, dst_ref=halo.at[stage, 1, rows],
            send_sem=halo_send.at[stage, 1, c], recv_sem=halo_recv.at[stage, 1, c],
            device_id=(rung, left), device_id_type=MESH,
        )
        up = pltpu.make_async_remote_copy(
            src_ref=high, dst_ref=halo.at[stage, 0, rows],
            send_sem=halo_send.at[stage, 0, c], recv_sem=halo_recv.at[stage, 0, c],
            device_id=(rung, right), device_id_type=MESH,
        )
        return down, up

    def swap_copy(which, c):
        rows = span(c)
        src = fb.at[LEAPS, :, rows] if which == 0 else pb.at[:, rows]
        dst = got_f if which == 0 else got_p
        return pltpu.make_async_remote_copy(
            src_ref=src, dst_ref=dst.at[:, rows],
            send_sem=swap_send.at[which, c], recv_sem=swap_recv.at[which, c],
            device_id=(mate, me), device_id_type=MESH,
        )

    def first_halo(c, carry):
        for copy in halo_copies(0, c):
            copy.start()
        return carry

    lax.fori_loop(0, chunks, first_halo, 0)

    acc[...] = jnp.zeros_like(acc)
    kappa = kappas[rung]
    lane = lax.broadcasted_iota(jnp.int32, (8, LANES), 1)
    slot = lane % NT
    row = lax.broadcasted_iota(jnp.int32, (8, width), 0)

    for load in loads:
        load.wait()

    def unit(stage, c):
        for copy in halo_copies(stage, c):
            copy.wait_recv()
        scale = STEP if 0 < stage < LEAPS else 0.5 * STEP
        of_sum = (2.0 * scale) * kappa

        def group(g, carry):
            base = c * ROWS + g * 8
            at = pl.ds(pl.multiple_of(base, 8), 8)
            before = pl.ds(pl.multiple_of(lax.rem(base + height - 8, height), 8), 8)
            after = pl.ds(pl.multiple_of(lax.rem(base + 8, height), 8), 8)
            hop = pot = kin = None
            for x in range(planes):
                cur = fb[stage, x, at, :]
                below = fb[stage, x - 1, at, :] if x > 0 else halo[stage, 0, at, :]
                above = fb[stage, x + 1, at, :] if x < planes - 1 else halo[stage, 1, at, :]
                up = pltpu.roll(jnp.where(row == 7, fb[stage, x, before, :], cur), 1, 0)
                down = pltpu.roll(jnp.where(row == 0, fb[stage, x, after, :], cur), 7, 0)
                total = (below + above) + (up + down) + zt_sum(cur, lane, slot)
                square = cur * cur
                moment = pb[x, at, :]
                fresh = moment + of_sum * total - (2.0 * scale) * (square * cur)
                pb[x, at, :] = fresh
                if stage < LEAPS:
                    fb[stage + 1, x, at, :] = cur + STEP * fresh
                if stage == 0 or stage == LEAPS:
                    kept = moment if stage == 0 else fresh
                    parts = (fold(cur * total), fold(square * square), fold(kept * kept))
                    if hop is None:
                        hop, pot, kin = parts
                    else:
                        hop, pot, kin = hop + parts[0], pot + parts[1], kin + parts[2]
            if stage == 0 or stage == LEAPS:
                first = 0 if stage == 0 else 3
                acc[first] += hop
                acc[first + 1] += pot
                acc[first + 2] += kin
            return carry

        lax.fori_loop(0, ROWS // 8, group, 0)
        if stage < LEAPS:
            for copy in halo_copies(stage + 1, c):
                copy.start()
        if stage >= LEAPS - 1:
            when_paired(lambda: swap_copy(stage - LEAPS + 1, c).start())

    def iteration(i, carry):
        for stage in range(STAGES):
            k = i - LAG * stage

            @pl.when((k >= 0) & (k < chunks))
            def _(stage=stage, k=k):
                unit(stage, lax.rem(stage + k, chunks))

        return carry

    lax.fori_loop(0, chunks + LAG * LEAPS, iteration, 0)

    volume = float(planes * ring * height * width)
    for j in range(6):
        part = jnp.sum(jnp.sum(acc[j], axis=0, keepdims=True), axis=1, keepdims=True)
        own[j : j + 1, :] = jnp.broadcast_to(part, (1, LANES))
    own[6:8, :] = jnp.zeros((2, LANES), jnp.float32)
    gx_buf[me] = own[...]

    def gx_copy(source, target):
        return pltpu.make_async_remote_copy(
            src_ref=own, dst_ref=gx_buf.at[source],
            send_sem=gx_send.at[target], recv_sem=gx_recv.at[source],
            device_id=(rung, target), device_id_type=MESH,
        )

    for off in range(1, ring):
        gx_copy(me, lax.rem(me + off, ring)).start()
    for off in range(1, ring):
        there = lax.rem(me + off, ring)
        gx_copy(there, there).wait_recv()
    total = gx_buf[0]
    for i in range(1, ring):
        total = total + gx_buf[i]
    rung_buf[rung] = total

    def rung_copy(source, target):
        return pltpu.make_async_remote_copy(
            src_ref=rung_buf.at[rung], dst_ref=rung_buf.at[source],
            send_sem=rung_send.at[target], recv_sem=rung_recv.at[source],
            device_id=(target, me), device_id_type=MESH,
        )

    for off in range(1, rungs):
        rung_copy(rung, lax.rem(rung + off, rungs)).start()

    swaps = partner[rung] != rung

    def out_copy(which, c, source):
        rows = span(c)
        dst = field_out if which == 0 else momenta_out
        return pltpu.make_async_copy(source.at[:, rows], dst.at[0, :, rows], out_sem.at[which, c])

    def settle(which, c):
        got = got_f if which == 0 else got_p
        rows = span(c)

        def arrived():
            swap_copy(which, c).wait_recv()
            mine = fb[LEAPS, :, rows, :] if which == 0 else pb[:, rows, :]
            got[:, rows, :] = jnp.where(swaps, got[:, rows, :], mine)

        def alone():
            got[:, rows, :] = fb[LEAPS, :, rows, :] if which == 0 else pb[:, rows, :]

        if odd:
            pl.when(paired)(arrived)
            pl.when(jnp.logical_not(paired))(alone)
        else:
            arrived()
        out_copy(which, c, got).start()

    def finish(k, carry):
        for which in range(2):
            settle(which, lax.rem(LEAPS - 1 + which + k, chunks))
        return carry

    lax.fori_loop(0, chunks, finish, 0)

    for off in range(1, rungs):
        there = lax.rem(rung + off, rungs)
        rung_copy(there, there).wait_recv()
    width_of = jnp.full((1, LANES), kappas[rungs - 1] - kappas[0], jnp.float32)
    cumulative = jnp.zeros((1, LANES), jnp.float32)
    for j in range(rungs - 1):
        gap = kappas[j + 1] - kappas[j]
        term = 2.0 * (rung_buf[j][3:4, :] * (0.5 / volume)) * gap / width_of
        cumulative = cumulative + jnp.where(rung >= j, term, jnp.zeros_like(term))
    mean = total * (1.0 / volume)
    energy = 0.5 * mean[2:3, :] + (0.5 * mean[1:2, :] + 0.5) - kappa * mean[0:1, :]
    spot = lax.broadcasted_iota(jnp.int32, (1, LANES), 1)
    line = jnp.where(spot == 0, 0.5 * mean[3:4, :], 0.5 * mean[4:5, :] + 0.5)
    line = jnp.where(spot == 2, 0.5 * mean[5:6, :], line)
    line = jnp.where(spot == 3, energy, line)
    line = jnp.where(spot == 4, cumulative, line)
    stats[...] = line[:, 0:5]

    def close(c, carry):
        for stage in range(STAGES):
            for copy in halo_copies(stage, c):
                copy.wait_send()
        for which in range(2):
            when_paired(lambda which=which: swap_copy(which, c).wait_send())
            out_copy(which, c, got_f if which == 0 else got_p).wait()
        return carry

    lax.fori_loop(0, chunks, close, 0)
    for off in range(1, ring):
        gx_copy(me, lax.rem(me + off, ring)).wait_send()
    for off in range(1, rungs):
        rung_copy(rung, lax.rem(rung + off, rungs)).wait_send()


def step(odd, kappas, partner, field, momenta):
    ring, rungs = lax.axis_size("gx"), lax.axis_size("ladder")
    _, planes, height, width = field.shape
    chunks = height // ROWS
    f32 = jnp.float32
    slab = (planes, height, width)
    dma = pltpu.SemaphoreType.DMA
    sites = planes * height * width
    return pl.pallas_call(
        functools.partial(body, odd, ring, rungs),
        out_shape=[
            jax.ShapeDtypeStruct(field.shape, f32),
            jax.ShapeDtypeStruct(field.shape, f32),
            jax.ShapeDtypeStruct((1, 5), f32),
        ],
        in_specs=[pl.BlockSpec(memory_space=pltpu.SMEM)] * 2 + [pl.BlockSpec(memory_space=pl.ANY)] * 2,
        out_specs=[pl.BlockSpec(memory_space=pl.ANY)] * 2 + [pl.BlockSpec(memory_space=pltpu.VMEM)],
        scratch_shapes=[
            pltpu.VMEM((STAGES,) + slab, f32),
            pltpu.VMEM(slab, f32),
            pltpu.VMEM((STAGES, 2, height, width), f32),
            pltpu.VMEM(slab, f32),
            pltpu.VMEM(slab, f32),
            pltpu.VMEM((6, 8, LANES), f32),
            pltpu.VMEM((8, LANES), f32),
            pltpu.VMEM((ring, 8, LANES), f32),
            pltpu.VMEM((rungs, 8, LANES), f32),
            dma((2,)),
            dma((STAGES, 2, chunks)),
            dma((STAGES, 2, chunks)),
            dma((2, chunks)),
            dma((2, chunks)),
            dma((2, chunks)),
            dma((ring,)),
            dma((ring,)),
            dma((rungs,)),
            dma((rungs,)),
        ],
        compiler_params=pltpu.CompilerParams(
            collective_id=odd, has_side_effects=True, vmem_limit_bytes=48 * 2**20
        ),
        cost_estimate=pl.CostEstimate(flops=150 * sites, bytes_accessed=16 * sites, transcendentals=0),
        name="odd_pairs" if odd else "even_pairs",
    )(kappas, partner, field, momenta)


def per_device(field, momenta, kappas, partner):
    place = jnp.arange(partner.shape[0], dtype=jnp.int32)
    odd = jnp.any((partner == place + 1) & (place % 2 == 1))
    return tuple(
        lax.cond(
            odd, functools.partial(step, 1), functools.partial(step, 0), kappas, partner, field, momenta
        )
    )


def solution(mesh):
    in_specs = (P("ladder", "gx", None, None), P("ladder", "gx", None, None), P(), P())
    out_specs = (P("ladder", "gx", None, None), P("ladder", "gx", None, None), P("ladder", None))
    return jax.shard_map(
        per_device, mesh=mesh, in_specs=in_specs, out_specs=out_specs, check_vma=False
    )
```

```python
import functools

import jax
import jax.numpy as jnp
from jax import lax
from jax.experimental import pallas as pl
from jax.experimental.pallas import tpu as pltpu
from jax.sharding import PartitionSpec as P

NT = 8
LEAPS = 4
LAMBDA = 0.5
STEP = 0.1

ROWS = 8
LAG = 2
STAGES = LEAPS + 1
LANES = 128
MESH = pl.DeviceIdType.MESH


def shifted_t(tile, slot):
    ahead = jnp.where(slot == NT - 1, pltpu.roll(tile, NT - 1, 1), pltpu.roll(tile, LANES - 1, 1))
    behind = jnp.where(slot == 0, pltpu.roll(tile, LANES - NT + 1, 1), pltpu.roll(tile, 1, 1))
    return ahead + behind


def zt_sum(cur, lane, slot):
    count = cur.shape[1] // LANES
    tiles = [cur[:, k * LANES : (k + 1) * LANES] for k in range(count)]
    up = [pltpu.roll(t, NT, 1) for t in tiles]
    down = [pltpu.roll(t, LANES - NT, 1) for t in tiles]
    sums = []
    for k in range(count):
        below = jnp.where(lane < NT, up[k - 1], up[k])
        above = jnp.where(lane >= LANES - NT, down[(k + 1) % count], down[k])
        sums.append(below + above + shifted_t(tiles[k], slot))
    return jnp.concatenate(sums, axis=1)


def fold(block):
    total = block[:, :LANES]
    for k in range(1, block.shape[1] // LANES):
        total = total + block[:, k * LANES : (k + 1) * LANES]
    return total


def body(
    odd, ring, rungs, kappas, partner, field, momenta,
    field_out, momenta_out, stats,
    fb, pb, halo, got_f, got_p, acc, own, gx_buf, rung_buf,
    load_sem, halo_send, halo_recv, swap_send, swap_recv, out_sem,
    gx_send, gx_recv, rung_send, rung_recv,
):
    planes, height, width = pb.shape
    chunks = height // ROWS
    rung = lax.axis_index("ladder")
    me = lax.axis_index("gx")
    right = lax.rem(me + 1, ring)
    left = lax.rem(me + ring - 1, ring)
    even_place = lax.rem(rung, 2) == 0
    if odd:
        paired = (rung > 0) & (rung < rungs - 1)
        mate = jnp.where(even_place, rung - 1, rung + 1)
        mate = jnp.where(paired, mate, rung)
    else:
        paired = None
        mate = jnp.where(even_place, rung + 1, rung - 1)

    def when_paired(todo):
        if odd:
            pl.when(paired)(todo)
        else:
            todo()

    loads = [
        pltpu.make_async_copy(field.at[0], fb.at[0], load_sem.at[0]),
        pltpu.make_async_copy(momenta.at[0], pb, load_sem.at[1]),
    ]
    for load in loads:
        load.start()

    barrier = pltpu.get_barrier_semaphore()
    for off in range(1, ring):
        pl.semaphore_signal(barrier, inc=1, device_id=(rung, lax.rem(me + off, ring)), device_id_type=MESH)
    for off in range(1, rungs):
        pl.semaphore_signal(barrier, inc=1, device_id=(lax.rem(rung + off, rungs), me), device_id_type=MESH)
    pl.semaphore_wait(barrier, ring - 1 + rungs - 1)

    def span(c):
        return pl.ds(pl.multiple_of(c * ROWS, ROWS), ROWS)

    def halo_copies(stage, c):
        rows = span(c)
        if stage == 0:
            low, high = field.at[0, 0, rows], field.at[0, planes - 1, rows]
        else:
            low, high = fb.at[stage, 0, rows], fb.at[stage, planes - 1, rows]
        down = pltpu.make_async_remote_copy(
            src_ref=low, dst_ref=halo.at[stage, 1, rows],
            send_sem=halo_send.at[stage, 1, c], recv_sem=halo_recv.at[stage, 1, c],
            device_id=(rung, left), device_id_type=MESH,
        )
        up = pltpu.make_async_remote_copy(
            src_ref=high, dst_ref=halo.at[stage, 0, rows],
            send_sem=halo_send.at[stage, 0, c], recv_sem=halo_recv.at[stage, 0, c],
            device_id=(rung, right), device_id_type=MESH,
        )
        return down, up

    def swap_copy(which, c):
        rows = span(c)
        src = fb.at[LEAPS, :, rows] if which == 0 else pb.at[:, rows]
        dst = got_f if which == 0 else got_p
        return pltpu.make_async_remote_copy(
            src_ref=src, dst_ref=dst.at[:, rows],
            send_sem=swap_send.at[which, c], recv_sem=swap_recv.at[which, c],
            device_id=(mate, me), device_id_type=MESH,
        )

    def first_halo(c):
        for copy in halo_copies(0, c):
            copy.start()

    wedge = LAG * LEAPS - 1
    lax.fori_loop(0, wedge, lambda c, carry: (first_halo(c), carry)[1], 0)

    acc[...] = jnp.zeros_like(acc)
    kappa = kappas[rung]
    lane = lax.broadcasted_iota(jnp.int32, (8, LANES), 1)
    slot = lane % NT
    row = lax.broadcasted_iota(jnp.int32, (8, width), 0)

    for load in loads:
        load.wait()

    def unit(stage, c):
        for copy in halo_copies(stage, c):
            copy.wait_recv()
        scale = STEP if 0 < stage < LEAPS else 0.5 * STEP
        of_sum = (2.0 * scale) * kappa

        def group(g, carry):
            base = c * ROWS + g * 8
            at = pl.ds(pl.multiple_of(base, 8), 8)
            before = pl.ds(pl.multiple_of(lax.rem(base + height - 8, height), 8), 8)
            after = pl.ds(pl.multiple_of(lax.rem(base + 8, height), 8), 8)
            hop = pot = kin = None
            for x in range(planes):
                cur = fb[stage, x, at, :]
                below = fb[stage, x - 1, at, :] if x > 0 else halo[stage, 0, at, :]
                above = fb[stage, x + 1, at, :] if x < planes - 1 else halo[stage, 1, at, :]
                up = pltpu.roll(jnp.where(row == 7, fb[stage, x, before, :], cur), 1, 0)
                down = pltpu.roll(jnp.where(row == 0, fb[stage, x, after, :], cur), 7, 0)
                total = (below + above) + (up + down) + zt_sum(cur, lane, slot)
                square = cur * cur
                moment = pb[x, at, :]
                fresh = moment + of_sum * total - (2.0 * scale) * (square * cur)
                pb[x, at, :] = fresh
                if stage < LEAPS:
                    fb[stage + 1, x, at, :] = cur + STEP * fresh
                if stage == 0 or stage == LEAPS:
                    kept = moment if stage == 0 else fresh
                    parts = (fold(cur * total), fold(square * square), fold(kept * kept))
                    if hop is None:
                        hop, pot, kin = parts
                    else:
                        hop, pot, kin = hop + parts[0], pot + parts[1], kin + parts[2]
            if stage == 0 or stage == LEAPS:
                first = 0 if stage == 0 else 3
                acc[first] += hop
                acc[first + 1] += pot
                acc[first + 2] += kin
            return carry

        lax.fori_loop(0, ROWS // 8, group, 0)
        if stage < LEAPS:
            for copy in halo_copies(stage + 1, c):
                copy.start()
        if stage >= LEAPS - 1:
            when_paired(lambda: swap_copy(stage - LEAPS + 1, c).start())

    for stage in range(LEAPS):
        if stage == LEAPS // 2:
            for c in range(wedge, min(wedge + LAG, chunks)):
                first_halo(c)
        lax.fori_loop(
            0, wedge - LAG * stage, lambda k, carry, stage=stage: (unit(stage, stage + k), carry)[1], 0
        )

    def iteration(i, carry):
        pl.when(i + LAG < chunks)(lambda: first_halo(i + LAG))
        for stage in range(STAGES):
            k = i - LAG * stage

            @pl.when((k >= 0) & (k < chunks))
            def _(stage=stage, k=k):
                unit(stage, lax.rem(stage + k, chunks))

        return carry

    lax.fori_loop(wedge, chunks + LAG * LEAPS, iteration, 0)

    volume = float(planes * ring * height * width)
    for j in range(6):
        part = jnp.sum(jnp.sum(acc[j], axis=0, keepdims=True), axis=1, keepdims=True)
        own[j : j + 1, :] = jnp.broadcast_to(part, (1, LANES))
    own[6:8, :] = jnp.zeros((2, LANES), jnp.float32)
    gx_buf[me] = own[...]

    def gx_copy(source, target):
        return pltpu.make_async_remote_copy(
            src_ref=own, dst_ref=gx_buf.at[source],
            send_sem=gx_send.at[target], recv_sem=gx_recv.at[source],
            device_id=(rung, target), device_id_type=MESH,
        )

    for off in range(1, ring):
        gx_copy(me, lax.rem(me + off, ring)).start()
    for off in range(1, ring):
        there = lax.rem(me + off, ring)
        gx_copy(there, there).wait_recv()
    total = gx_buf[0]
    for i in range(1, ring):
        total = total + gx_buf[i]
    rung_buf[rung] = total

    def rung_copy(source, target):
        return pltpu.make_async_remote_copy(
            src_ref=rung_buf.at[rung], dst_ref=rung_buf.at[source],
            send_sem=rung_send.at[target], recv_sem=rung_recv.at[source],
            device_id=(target, me), device_id_type=MESH,
        )

    for off in range(1, rungs):
        rung_copy(rung, lax.rem(rung + off, rungs)).start()

    swaps = partner[rung] != rung

    def out_copy(which, c, source):
        rows = span(c)
        dst = field_out if which == 0 else momenta_out
        return pltpu.make_async_copy(source.at[:, rows], dst.at[0, :, rows], out_sem.at[which, c])

    def settle(which, c):
        got = got_f if which == 0 else got_p
        rows = span(c)

        def arrived():
            swap_copy(which, c).wait_recv()
            mine = fb[LEAPS, :, rows, :] if which == 0 else pb[:, rows, :]
            got[:, rows, :] = jnp.where(swaps, got[:, rows, :], mine)

        def alone():
            got[:, rows, :] = fb[LEAPS, :, rows, :] if which == 0 else pb[:, rows, :]

        if odd:
            pl.when(paired)(arrived)
            pl.when(jnp.logical_not(paired))(alone)
        else:
            arrived()
        out_copy(which, c, got).start()

    def finish(k, carry):
        for which in range(2):
            settle(which, lax.rem(LEAPS - 1 + which + k, chunks))
        return carry

    lax.fori_loop(0, chunks, finish, 0)

    for off in range(1, rungs):
        there = lax.rem(rung + off, rungs)
        rung_copy(there, there).wait_recv()
    width_of = jnp.full((1, LANES), kappas[rungs - 1] - kappas[0], jnp.float32)
    cumulative = jnp.zeros((1, LANES), jnp.float32)
    for j in range(rungs - 1):
        gap = kappas[j + 1] - kappas[j]
        term = 2.0 * (rung_buf[j][3:4, :] * (0.5 / volume)) * gap / width_of
        cumulative = cumulative + jnp.where(rung >= j, term, jnp.zeros_like(term))
    mean = total * (1.0 / volume)
    energy = 0.5 * mean[2:3, :] + (0.5 * mean[1:2, :] + 0.5) - kappa * mean[0:1, :]
    spot = lax.broadcasted_iota(jnp.int32, (1, LANES), 1)
    line = jnp.where(spot == 0, 0.5 * mean[3:4, :], 0.5 * mean[4:5, :] + 0.5)
    line = jnp.where(spot == 2, 0.5 * mean[5:6, :], line)
    line = jnp.where(spot == 3, energy, line)
    line = jnp.where(spot == 4, cumulative, line)
    stats[...] = line[:, 0:5]

    def close(c, carry):
        for stage in range(STAGES):
            for copy in halo_copies(stage, c):
                copy.wait_send()
        for which in range(2):
            when_paired(lambda which=which: swap_copy(which, c).wait_send())
            out_copy(which, c, got_f if which == 0 else got_p).wait()
        return carry

    lax.fori_loop(0, chunks, close, 0)
    for off in range(1, ring):
        gx_copy(me, lax.rem(me + off, ring)).wait_send()
    for off in range(1, rungs):
        rung_copy(rung, lax.rem(rung + off, rungs)).wait_send()


def step(odd, kappas, partner, field, momenta):
    ring, rungs = lax.axis_size("gx"), lax.axis_size("ladder")
    _, planes, height, width = field.shape
    chunks = height // ROWS
    f32 = jnp.float32
    slab = (planes, height, width)
    dma = pltpu.SemaphoreType.DMA
    sites = planes * height * width
    return pl.pallas_call(
        functools.partial(body, odd, ring, rungs),
        out_shape=[
            jax.ShapeDtypeStruct(field.shape, f32),
            jax.ShapeDtypeStruct(field.shape, f32),
            jax.ShapeDtypeStruct((1, 5), f32),
        ],
        in_specs=[pl.BlockSpec(memory_space=pltpu.SMEM)] * 2 + [pl.BlockSpec(memory_space=pl.ANY)] * 2,
        out_specs=[pl.BlockSpec(memory_space=pl.ANY)] * 2 + [pl.BlockSpec(memory_space=pltpu.VMEM)],
        scratch_shapes=[
            pltpu.VMEM((STAGES,) + slab, f32),
            pltpu.VMEM(slab, f32),
            pltpu.VMEM((STAGES, 2, height, width), f32),
            pltpu.VMEM(slab, f32),
            pltpu.VMEM(slab, f32),
            pltpu.VMEM((6, 8, LANES), f32),
            pltpu.VMEM((8, LANES), f32),
            pltpu.VMEM((ring, 8, LANES), f32),
            pltpu.VMEM((rungs, 8, LANES), f32),
            dma((2,)),
            dma((STAGES, 2, chunks)),
            dma((STAGES, 2, chunks)),
            dma((2, chunks)),
            dma((2, chunks)),
            dma((2, chunks)),
            dma((ring,)),
            dma((ring,)),
            dma((rungs,)),
            dma((rungs,)),
        ],
        compiler_params=pltpu.CompilerParams(
            collective_id=odd, has_side_effects=True, vmem_limit_bytes=48 * 2**20
        ),
        cost_estimate=pl.CostEstimate(flops=150 * sites, bytes_accessed=16 * sites, transcendentals=0),
        name="odd_pairs" if odd else "even_pairs",
    )(kappas, partner, field, momenta)


def per_device(field, momenta, kappas, partner):
    place = jnp.arange(partner.shape[0], dtype=jnp.int32)
    odd = jnp.any((partner == place + 1) & (place % 2 == 1))
    return tuple(
        lax.cond(
            odd, functools.partial(step, 1), functools.partial(step, 0), kappas, partner, field, momenta
        )
    )


def solution(mesh):
    in_specs = (P("ladder", "gx", None, None), P("ladder", "gx", None, None), P(), P())
    out_specs = (P("ladder", "gx", None, None), P("ladder", "gx", None, None), P("ladder", None))
    return jax.shard_map(
        per_device, mesh=mesh, in_specs=in_specs, out_specs=out_specs, check_vma=False
    )
```

```python
import functools

import jax
import jax.numpy as jnp
from jax import lax
from jax.experimental import pallas as pl
from jax.experimental.pallas import tpu as pltpu
from jax.sharding import PartitionSpec as P

NT = 8
LEAPS = 4
LAMBDA = 0.5
STEP = 0.1

ROWS = 8
LAG = 2
STAGES = LEAPS + 1
LANES = 128
MESH = pl.DeviceIdType.MESH


def shifted_t(tile, slot):
    ahead = jnp.where(slot == NT - 1, pltpu.roll(tile, NT - 1, 1), pltpu.roll(tile, LANES - 1, 1))
    behind = jnp.where(slot == 0, pltpu.roll(tile, LANES - NT + 1, 1), pltpu.roll(tile, 1, 1))
    return ahead + behind


def zt_sum(cur, lane, slot):
    count = cur.shape[1] // LANES
    tiles = [cur[:, k * LANES : (k + 1) * LANES] for k in range(count)]
    up = [pltpu.roll(t, NT, 1) for t in tiles]
    down = [pltpu.roll(t, LANES - NT, 1) for t in tiles]
    sums = []
    for k in range(count):
        below = jnp.where(lane < NT, up[k - 1], up[k])
        above = jnp.where(lane >= LANES - NT, down[(k + 1) % count], down[k])
        sums.append(below + above + shifted_t(tiles[k], slot))
    return jnp.concatenate(sums, axis=1)


def fold(block):
    total = block[:, :LANES]
    for k in range(1, block.shape[1] // LANES):
        total = total + block[:, k * LANES : (k + 1) * LANES]
    return total


def body(
    odd, ring, rungs, kappas, partner, field, momenta,
    field_out, momenta_out, stats,
    fb, pb, halo, got_f, got_p, acc, own, gx_buf, rung_buf,
    load_sem, halo_send, halo_recv, swap_send, swap_recv, out_sem,
    gx_send, gx_recv, rung_send, rung_recv,
):
    planes, height, width = pb.shape
    chunks = height // ROWS
    rung = lax.axis_index("ladder")
    me = lax.axis_index("gx")
    right = lax.rem(me + 1, ring)
    left = lax.rem(me + ring - 1, ring)
    even_place = lax.rem(rung, 2) == 0
    if odd:
        paired = (rung > 0) & (rung < rungs - 1)
        mate = jnp.where(even_place, rung - 1, rung + 1)
        mate = jnp.where(paired, mate, rung)
    else:
        paired = None
        mate = jnp.where(even_place, rung + 1, rung - 1)

    def when_paired(todo):
        if odd:
            pl.when(paired)(todo)
        else:
            todo()

    loads = [
        pltpu.make_async_copy(field.at[0], fb.at[0], load_sem.at[0]),
        pltpu.make_async_copy(momenta.at[0], pb, load_sem.at[1]),
    ]
    for load in loads:
        load.start()

    barrier = pltpu.get_barrier_semaphore()
    for off in range(1, ring):
        pl.semaphore_signal(barrier, inc=1, device_id=(rung, lax.rem(me + off, ring)), device_id_type=MESH)
    for off in range(1, rungs):
        pl.semaphore_signal(barrier, inc=1, device_id=(lax.rem(rung + off, rungs), me), device_id_type=MESH)
    pl.semaphore_wait(barrier, ring - 1 + rungs - 1)

    def span(c):
        return pl.ds(pl.multiple_of(c * ROWS, ROWS), ROWS)

    def halo_copies(stage, c):
        rows = span(c)
        if stage == 0:
            low, high = field.at[0, 0, rows], field.at[0, planes - 1, rows]
        else:
            low, high = fb.at[stage, 0, rows], fb.at[stage, planes - 1, rows]
        down = pltpu.make_async_remote_copy(
            src_ref=low, dst_ref=halo.at[stage, 1, rows],
            send_sem=halo_send.at[stage, 1, c], recv_sem=halo_recv.at[stage, 1, c],
            device_id=(rung, left), device_id_type=MESH,
        )
        up = pltpu.make_async_remote_copy(
            src_ref=high, dst_ref=halo.at[stage, 0, rows],
            send_sem=halo_send.at[stage, 0, c], recv_sem=halo_recv.at[stage, 0, c],
            device_id=(rung, right), device_id_type=MESH,
        )
        return down, up

    def swap_copy(which, c):
        rows = span(c)
        src = fb.at[LEAPS, :, rows] if which == 0 else pb.at[:, rows]
        dst = got_f if which == 0 else got_p
        return pltpu.make_async_remote_copy(
            src_ref=src, dst_ref=dst.at[:, rows],
            send_sem=swap_send.at[which, c], recv_sem=swap_recv.at[which, c],
            device_id=(mate, me), device_id_type=MESH,
        )

    def first_halo(c):
        for copy in halo_copies(0, c):
            copy.start()

    wedge = LAG * LEAPS - 1
    lax.fori_loop(0, wedge, lambda c, carry: (first_halo(c), carry)[1], 0)

    acc[...] = jnp.zeros_like(acc)
    kappa = kappas[rung]
    lane = lax.broadcasted_iota(jnp.int32, (8, LANES), 1)
    slot = lane % NT
    row = lax.broadcasted_iota(jnp.int32, (8, width), 0)

    for load in loads:
        load.wait()

    def unit(stage, c):
        for copy in halo_copies(stage, c):
            copy.wait_recv()
        scale = STEP if 0 < stage < LEAPS else 0.5 * STEP
        of_sum = (2.0 * scale) * kappa

        def group(g, carry):
            base = c * ROWS + g * 8
            at = pl.ds(pl.multiple_of(base, 8), 8)
            before = pl.ds(pl.multiple_of(lax.rem(base + height - 8, height), 8), 8)
            after = pl.ds(pl.multiple_of(lax.rem(base + 8, height), 8), 8)
            hop = pot = kin = None
            for x in range(planes):
                cur = fb[stage, x, at, :]
                below = fb[stage, x - 1, at, :] if x > 0 else halo[stage, 0, at, :]
                above = fb[stage, x + 1, at, :] if x < planes - 1 else halo[stage, 1, at, :]
                up = pltpu.roll(jnp.where(row == 7, fb[stage, x, before, :], cur), 1, 0)
                down = pltpu.roll(jnp.where(row == 0, fb[stage, x, after, :], cur), 7, 0)
                total = (below + above) + (up + down) + zt_sum(cur, lane, slot)
                square = cur * cur
                moment = pb[x, at, :]
                fresh = moment + of_sum * total - (2.0 * scale) * (square * cur)
                pb[x, at, :] = fresh
                if stage < LEAPS:
                    fb[stage + 1, x, at, :] = cur + STEP * fresh
                if stage == 0 or stage == LEAPS:
                    kept = moment if stage == 0 else fresh
                    parts = (fold(cur * total), fold(square * square), fold(kept * kept))
                    if hop is None:
                        hop, pot, kin = parts
                    else:
                        hop, pot, kin = hop + parts[0], pot + parts[1], kin + parts[2]
            if stage == 0 or stage == LEAPS:
                first = 0 if stage == 0 else 3
                acc[first] += hop
                acc[first + 1] += pot
                acc[first + 2] += kin
            return carry

        lax.fori_loop(0, ROWS // 8, group, 0)
        if stage < LEAPS:
            for copy in halo_copies(stage + 1, c):
                copy.start()
        if stage >= LEAPS - 1:
            when_paired(lambda: swap_copy(stage - LEAPS + 1, c).start())

    for stage in range(LEAPS):
        if stage == LEAPS // 2:
            for c in range(wedge, min(wedge + LAG, chunks)):
                first_halo(c)
        lax.fori_loop(
            0, wedge - LAG * stage, lambda k, carry, stage=stage: (unit(stage, stage + k), carry)[1], 0
        )

    def iteration(i, carry):
        pl.when(i + LAG < chunks)(lambda: first_halo(i + LAG))
        for stage in range(STAGES):
            k = i - LAG * stage

            @pl.when((k >= 0) & (k < chunks))
            def _(stage=stage, k=k):
                unit(stage, lax.rem(stage + k, chunks))

        return carry

    lax.fori_loop(wedge, chunks + LAG * LEAPS, iteration, 0)

    volume = float(planes * ring * height * width)
    for j in range(6):
        part = jnp.sum(jnp.sum(acc[j], axis=0, keepdims=True), axis=1, keepdims=True)
        own[j : j + 1, :] = jnp.broadcast_to(part, (1, LANES))
    own[6:8, :] = jnp.zeros((2, LANES), jnp.float32)
    gx_buf[me] = own[...]

    def gx_copy(source, target):
        return pltpu.make_async_remote_copy(
            src_ref=own, dst_ref=gx_buf.at[source],
            send_sem=gx_send.at[target], recv_sem=gx_recv.at[source],
            device_id=(rung, target), device_id_type=MESH,
        )

    for off in range(1, ring):
        gx_copy(me, lax.rem(me + off, ring)).start()
    for off in range(1, ring):
        there = lax.rem(me + off, ring)
        gx_copy(there, there).wait_recv()
    total = gx_buf[0]
    for i in range(1, ring):
        total = total + gx_buf[i]
    rung_buf[rung] = total

    def rung_copy(source, target):
        return pltpu.make_async_remote_copy(
            src_ref=rung_buf.at[rung], dst_ref=rung_buf.at[source],
            send_sem=rung_send.at[target], recv_sem=rung_recv.at[source],
            device_id=(target, me), device_id_type=MESH,
        )

    for off in range(1, rungs):
        rung_copy(rung, lax.rem(rung + off, rungs)).start()

    swaps = partner[rung] != rung

    def out_copy(which, c, source):
        rows = span(c)
        dst = field_out if which == 0 else momenta_out
        return pltpu.make_async_copy(source.at[:, rows], dst.at[0, :, rows], out_sem.at[which, c])

    def settle(which, c):
        got = got_f if which == 0 else got_p
        rows = span(c)

        def arrived():
            swap_copy(which, c).wait_recv()
            mine = fb[LEAPS, :, rows, :] if which == 0 else pb[:, rows, :]
            got[:, rows, :] = jnp.where(swaps, got[:, rows, :], mine)

        def alone():
            got[:, rows, :] = fb[LEAPS, :, rows, :] if which == 0 else pb[:, rows, :]

        if odd:
            pl.when(paired)(arrived)
            pl.when(jnp.logical_not(paired))(alone)
        else:
            arrived()
        out_copy(which, c, got).start()

    def written(which, k):
        c = lax.rem(LEAPS - 1 + which + k, chunks)
        out_copy(which, c, got_f if which == 0 else got_p).wait()

    def finish(k, carry):
        for which in range(2):
            c = lax.rem(LEAPS - 1 + which + k, chunks)
            settle(which, c)
            when_paired(lambda which=which, c=c: swap_copy(which, c).wait_send())
            pl.when(k > 0)(lambda which=which, k=k: written(which, k - 1))
        return carry

    def close(c, carry):
        for stage in range(STAGES):
            for copy in halo_copies(stage, c):
                copy.wait_send()
        return carry

    lax.fori_loop(0, chunks, close, 0)
    lax.fori_loop(0, chunks - 2, finish, 0)

    for off in range(1, rungs):
        there = lax.rem(rung + off, rungs)
        rung_copy(there, there).wait_recv()
    width_of = jnp.full((1, LANES), kappas[rungs - 1] - kappas[0], jnp.float32)
    cumulative = jnp.zeros((1, LANES), jnp.float32)
    for j in range(rungs - 1):
        gap = kappas[j + 1] - kappas[j]
        term = 2.0 * (rung_buf[j][3:4, :] * (0.5 / volume)) * gap / width_of
        cumulative = cumulative + jnp.where(rung >= j, term, jnp.zeros_like(term))
    mean = total * (1.0 / volume)
    energy = 0.5 * mean[2:3, :] + (0.5 * mean[1:2, :] + 0.5) - kappa * mean[0:1, :]
    spot = lax.broadcasted_iota(jnp.int32, (1, LANES), 1)
    line = jnp.where(spot == 0, 0.5 * mean[3:4, :], 0.5 * mean[4:5, :] + 0.5)
    line = jnp.where(spot == 2, 0.5 * mean[5:6, :], line)
    line = jnp.where(spot == 3, energy, line)
    line = jnp.where(spot == 4, cumulative, line)
    stats[...] = line[:, 0:5]

    for off in range(1, ring):
        gx_copy(me, lax.rem(me + off, ring)).wait_send()
    for off in range(1, rungs):
        rung_copy(rung, lax.rem(rung + off, rungs)).wait_send()
    lax.fori_loop(chunks - 2, chunks, finish, 0)
    for which in range(2):
        written(which, chunks - 1)


def step(odd, kappas, partner, field, momenta):
    ring, rungs = lax.axis_size("gx"), lax.axis_size("ladder")
    _, planes, height, width = field.shape
    chunks = height // ROWS
    f32 = jnp.float32
    slab = (planes, height, width)
    dma = pltpu.SemaphoreType.DMA
    sites = planes * height * width
    return pl.pallas_call(
        functools.partial(body, odd, ring, rungs),
        out_shape=[
            jax.ShapeDtypeStruct(field.shape, f32),
            jax.ShapeDtypeStruct(field.shape, f32),
            jax.ShapeDtypeStruct((1, 5), f32),
        ],
        in_specs=[pl.BlockSpec(memory_space=pltpu.SMEM)] * 2 + [pl.BlockSpec(memory_space=pl.ANY)] * 2,
        out_specs=[pl.BlockSpec(memory_space=pl.ANY)] * 2 + [pl.BlockSpec(memory_space=pltpu.VMEM)],
        scratch_shapes=[
            pltpu.VMEM((STAGES,) + slab, f32),
            pltpu.VMEM(slab, f32),
            pltpu.VMEM((STAGES, 2, height, width), f32),
            pltpu.VMEM(slab, f32),
            pltpu.VMEM(slab, f32),
            pltpu.VMEM((6, 8, LANES), f32),
            pltpu.VMEM((8, LANES), f32),
            pltpu.VMEM((ring, 8, LANES), f32),
            pltpu.VMEM((rungs, 8, LANES), f32),
            dma((2,)),
            dma((STAGES, 2, chunks)),
            dma((STAGES, 2, chunks)),
            dma((2, chunks)),
            dma((2, chunks)),
            dma((2, chunks)),
            dma((ring,)),
            dma((ring,)),
            dma((rungs,)),
            dma((rungs,)),
        ],
        compiler_params=pltpu.CompilerParams(
            collective_id=odd, has_side_effects=True, vmem_limit_bytes=48 * 2**20
        ),
        cost_estimate=pl.CostEstimate(flops=150 * sites, bytes_accessed=16 * sites, transcendentals=0),
        name="odd_pairs" if odd else "even_pairs",
    )(kappas, partner, field, momenta)


def per_device(field, momenta, kappas, partner):
    place = jnp.arange(partner.shape[0], dtype=jnp.int32)
    odd = jnp.any((partner == place + 1) & (place % 2 == 1))
    return tuple(
        lax.cond(
            odd, functools.partial(step, 1), functools.partial(step, 0), kappas, partner, field, momenta
        )
    )


def solution(mesh):
    in_specs = (P("ladder", "gx", None, None), P("ladder", "gx", None, None), P(), P())
    out_specs = (P("ladder", "gx", None, None), P("ladder", "gx", None, None), P("ladder", None))
    return jax.shard_map(
        per_device, mesh=mesh, in_specs=in_specs, out_specs=out_specs, check_vma=False
    )
```
